256 devices in a mesh: inp: 8 (over z), wt: 8 (over x_lo, y), out: 4 (over x_hi, core).
Axes of the slice: x: 4 (x_hi: 2, x_lo: 2; x = x_hi * 2 + x_lo), y: 4, z: 8, core: 2. Of those that a mesh axis runs over, the one named last changes fastest.
Arguments:
- tokens: bfloat16 [1536, 8192], P(('inp', 'out'), 'wt'), may hold values from -6 to 6
- gate_weight: bfloat16 [8192, 28672], P('wt', ('inp', 'out')), may hold values from -0.0625 to 0.0625
- up_weight: bfloat16 [8192, 28672], P('wt', ('inp', 'out')), may hold values from -0.0625 to 0.0625
- down_weight: bfloat16 [28672, 8192], P(('inp', 'out'), 'wt'), may hold values from -0.03125 to 0.03125
Outputs:
- mixed: bfloat16 [1536, 8192], P(('inp', 'out'), 'wt')
The draws below stay inside these ranges and needn't reach their ends.
All inputs are finite; a program needn't handle non-finite values.
Results may differ from the reference program's by a relative error of at most 0.0049.
Values may be sent and summed in bfloat16 or wider, within the bound.
A program may use at most 128 MiB of HBM per device.

```python
import jax
import jax.numpy as jnp

D = 8192
FF = 28672
TOKENS = 1536


def block_levels(own_key, shape, cuts, smallest, largest):
    def one(position, parts):
        draws = jax.random.uniform(jax.random.fold_in(jax.random.fold_in(own_key, 6), position), (parts,), jnp.float32, smallest / len(cuts), largest / len(cuts))
        return jnp.repeat(jnp.exp(draws), shape[position] // parts).reshape((-1,) + (1,) * (len(shape) - position - 1))

    loudness = one(*cuts[0])
    for cut in cuts[1:]:
        loudness = loudness * one(*cut)
    return loudness


def normal_values(key, extent, width, reach, split=(), dtype=jnp.bfloat16):
    array = jax.random.normal(key, extent, jnp.float32) * width
    if len(split) > 0:
        array = block_levels(key, extent, split, -0.22, 0.18) * array
    return jnp.clip(array, min=-reach, max=reach).astype(dtype)


def setup_inputs(seed: int = 0) -> dict:
    key_of = jax.random.split(jax.random.key(seed), 5)
    tokens = normal_values(key_of[0], (TOKENS, D), 1.0, 6.0, ((0, 32), (1, 8)))
    gate_weight = normal_values(key_of[1], (D, FF), D ** -0.5, 0.0625, ((0, 8), (1, 32)))
    up_weight = normal_values(key_of[2], (D, FF), D ** -0.5, 0.0625, ((0, 8), (1, 32)))
    down_weight = normal_values(key_of[3], (FF, D), FF ** -0.5, 0.03125, ((0, 32), (1, 8)))
    return dict(tokens=tokens, gate_weight=gate_weight, up_weight=up_weight, down_weight=down_weight)


def reference(tokens, gate_weight, up_weight, down_weight):
    gate = jnp.dot(tokens, gate_weight, preferred_element_type=jnp.float32)
    up = jnp.dot(tokens, up_weight, preferred_element_type=jnp.float32)
    hidden = (gate * jax.nn.sigmoid(gate) * up).astype(jnp.bfloat16)
    return jnp.dot(hidden, down_weight, preferred_element_type=jnp.float32).astype(jnp.bfloat16)
```

```python
import jax
import jax.numpy as jnp
from jax import lax
from jax.experimental import pallas as pl
from jax.experimental.pallas import tpu as pltpu
from jax.sharding import PartitionSpec as P

MESH = pl.DeviceIdType.MESH
BF, F32 = jnp.bfloat16, jnp.float32

ROWS = 48
KB = 1024
FB = 896
HALF = 512
CHUNKS = 4
OFFS = ((0, 1), (-2, 3), (4, -3), (-1, 2))
STAGE_AT = dict(xf=-1.0, m1=0.0, s2=9.0, s3=14.0, s4=18.0, a2=21.0, a3=24.0, m2=27.0, g1=30.0)
CHUNK_AT = (0.0, 5.0, 18.0, 31.0)
N_SEM = 192


def kernel(tok, wg, wu, wd, out, w1, w2, x, p16, p32, gr1, sb, gr2, gs, gx, ux, q16, q32, ur1, uv, ur2, h, o32, cr, zs, zr, own,
           ssem, rsem, lsem):
    z = lax.axis_index("inp")
    wt = lax.axis_index("wt")
    ot = lax.axis_index("out")
    a, y = wt // 4, wt % 4
    xh, core = ot // 2, ot % 2
    na = 1 - a
    yr, yl, yo = (y + 1) % 4, (y + 3) % 4, (y + 2) % 4

    def dev(dz=0, dx=0, dc=0):
        return (lax.rem(z + dz + 8, 8), wt, (xh + dx) % 2 * 2 + (core + dc) % 2)

    sibling = dev(dc=1)
    right, left, across = (z, a * 4 + yr, ot), (z, a * 4 + yl, ot), (z, na * 4 + y, ot)

    loads = [
        pltpu.make_async_copy(tok, x.at[0, 0, 0, 0], lsem.at[0]),
        pltpu.make_async_copy(wg, w1.at[:, pl.ds(0, FB)], lsem.at[1]),
        pltpu.make_async_copy(wu, w1.at[:, pl.ds(FB, FB)], lsem.at[2]),
        pltpu.make_async_copy(wd, w2, lsem.at[3]),
    ]
    for load in loads:
        load.start()

    barrier = pltpu.get_barrier_semaphore()
    peers = [sibling, right, left, across]
    for dz in range(8):
        for dx in range(2):
            if dz or dx:
                peers.append(dev(dz=dz, dx=dx))
    for peer in peers:
        pl.semaphore_signal(barrier, inc=1, device_id=peer, device_id_type=MESH)
    pl.semaphore_wait(barrier, len(peers))

    copies = {}

    def send(name, src, dst, to):
        i = len(copies)
        cp = pltpu.make_async_remote_copy(
            src_ref=src, dst_ref=dst, send_sem=ssem.at[i], recv_sem=rsem.at[i], device_id=to, device_id_type=MESH
        )
        cp.start()
        copies[name] = cp

    def got(*names):
        for name in names:
            copies[name].wait_recv()

    loads[0].wait()
    send("x_hi", x.at[0, 0, 0, 0], x.at[0, 0, 1, 0], dev(dx=1))
    send("x_c0", x.at[0, 0, 0, 0], x.at[0, 0, 0, 1], sibling)
    got("x_hi")
    for c in range(CHUNKS):
        for zi in range(2):
            o = OFFS[c][zi]
            if o:
                send(("x", c, zi), x.at[0, 0, :, 0], x.at[c, zi, :, 0], dev(dz=-o))
    send("x_c1", x.at[0, 0, 1, 0], x.at[0, 0, 1, 1], sibling)

    def xf(c):
        for zi in range(2):
            if OFFS[c][zi]:
                got(("x", c, zi))
                send(("xc", c, zi), x.at[c, zi, :, 0], x.at[c, zi, :, 1], sibling)

    def m1(c):
        if c == 0:
            got("x_c0", "x_c1")
            loads[1].wait()
            loads[2].wait()
        for zi in range(2):
            if OFFS[c][zi]:
                got(("xc", c, zi))

        def tile(j, _):
            cols = pl.ds(pl.multiple_of(j * 256, 256), 256)
            r = jnp.dot(x[c].reshape(8 * ROWS, KB), w1[:, cols], preferred_element_type=F32)
            r = r.reshape(4, 2, ROWS, 256)
            p32[c, :, :, :, cols] = r
            p16[c, :, :, :, cols] = r.astype(BF)
            return 0

        lax.fori_loop(0, 7, tile, 0)
        g, u = pl.ds(0, FB), pl.ds(FB, FB)
        send(("u0", c), p16.at[c, :, na, :, u], ux.at[c], across)
        send(("g1r", c), p16.at[c, yo, 0, :, g], gr1.at[c, 0], right)
        send(("g1l", c), p16.at[c, yo, 1, :, g], gr1.at[c, 1], left)
        send(("g2r1", c), p16.at[c, yr, 1, :, g], gr2.at[c, 0, 1], right)
        send(("g2l0", c), p16.at[c, yl, 0, :, g], gr2.at[c, 1, 0], left)

    def s2(c):
        got(("g1r", c))
        sb[c, 0] = (p32[c, yr, 0, :, :FB] + gr1[c, 0].astype(F32)).astype(BF)
        send(("g2r0", c), sb.at[c, 0], gr2.at[c, 0, 0], right)
        got(("g1l", c))
        sb[c, 1] = (p32[c, yl, 1, :, :FB] + gr1[c, 1].astype(F32)).astype(BF)
        send(("g2l1", c), sb.at[c, 1], gr2.at[c, 1, 1], left)
        got(("u0", c))
        for k in range(4):
            q = p32[c, k, a, :, FB:] + ux[c, k].astype(F32)
            q32[c, k] = q
            q16[c, k] = q.astype(BF)
        lo, hi = pl.ds(0, HALF), pl.ds(HALF, FB - HALF)
        send(("u1r", c), q16.at[c, yo, :, lo], ur1.at[c, :, lo], right)
        send(("u1l", c), q16.at[c, yo, :, hi], ur1.at[c, :, hi], left)
        send(("u2rh", c), q16.at[c, yr, :, hi], ur2.at[c, 0, :, hi], right)
        send(("u2ll", c), q16.at[c, yl, :, lo], ur2.at[c, 1, :, lo], left)

    def s3(c):
        got(("g2r0", c), ("g2r1", c), ("g2l0", c), ("g2l1", c))
        t = p32[c, y, na, :, :FB] + gr2[c, 0, na].astype(F32) + gr2[c, 1, na].astype(F32)
        gs[c] = t.astype(BF)
        send(("gx", c), gs.at[c], gx.at[c], across)
        lo, hi = pl.ds(0, HALF), pl.ds(HALF, FB - HALF)
        got(("u1r", c))
        uv[c, :, :HALF] = (q32[c, yr, :, :HALF] + ur1[c, :, :HALF].astype(F32)).astype(BF)
        send(("u2rl", c), uv.at[c, :, lo], ur2.at[c, 0, :, lo], right)
        got(("u1l", c))
        uv[c, :, HALF:] = (q32[c, yl, :, HALF:] + ur1[c, :, HALF:].astype(F32)).astype(BF)
        send(("u2lh", c), uv.at[c, :, hi], ur2.at[c, 1, :, hi], left)

    def s4(c):
        got(("gx", c), ("u2rl", c), ("u2rh", c), ("u2ll", c), ("u2lh", c))
        gate = p32[c, y, a, :, :FB] + gr2[c, 0, a].astype(F32) + gr2[c, 1, a].astype(F32) + gx[c].astype(F32)
        up = q32[c, y] + ur2[c, 0].astype(F32) + ur2[c, 1].astype(F32)
        h[c, y, a] = (gate * jax.nn.sigmoid(gate) * up).astype(BF)
        send(("hx", c), h.at[c, y, a], h.at[c, y, a], across)
        send(("hr", c), h.at[c, y, a], h.at[c, y, a], right)
        send(("hl", c), h.at[c, y, a], h.at[c, y, a], left)

    def a2(c):
        got(("hx", c))
        send(("pr", c), h.at[c, y, na], h.at[c, y, na], right)
        send(("pl", c), h.at[c, y, na], h.at[c, y, na], left)

    def a3(c):
        got(("hr", c))
        send(("fr", c), h.at[c, yl, a], h.at[c, yl, a], right)
        got(("pl", c))
        send(("fl", c), h.at[c, yr, na], h.at[c, yr, na], left)

    def m2(c):
        if c == 0:
            loads[3].wait()
        got(("hl", c), ("pr", c), ("fr", c), ("fl", c))

        def tile(j, _):
            cols = pl.ds(pl.multiple_of(j * 256, 256), 256)
            r = jnp.dot(h[c].reshape(8 * ROWS, FB), w2[:, cols], preferred_element_type=F32)
            o32[c, :, :, :, cols] = r.reshape(4, 2, ROWS, 256)
            return 0

        lax.fori_loop(0, 4, tile, 0)
        send(("c", c), o32.at[c, :, 1], cr.at[c], sibling)

    def g1(c):
        got(("c", c))
        for zi in range(2):
            for dx in range(2):
                k = zi * 2 + dx
                v = o32[c, k, 0] + cr[c, k]
                if OFFS[c][zi] == 0 and dx == 0:
                    own[...] = v
                else:
                    zs[c, k] = v.astype(BF)
                    send(("z", c, k), zs.at[c, k], zr.at[c, k], dev(dz=OFFS[c][zi], dx=dx))

    stages = dict(xf=xf, m1=m1, s2=s2, s3=s3, s4=s4, a2=a2, a3=a3, m2=m2, g1=g1)
    order = sorted((CHUNK_AT[c] + at, c, s) for c in range(CHUNKS) for s, at in STAGE_AT.items())
    for _, c, s in order:
        with jax.named_scope(f"{s}_{c}"):
            stages[s](c)

    total = own[...]
    for c in range(CHUNKS):
        for k in range(4):
            if ("z", c, k) in copies:
                got(("z", c, k))
                total += zr[c, k].astype(F32)
    out[...] = total.astype(BF)
    for cp in copies.values():
        cp.wait_send()


def solution(mesh):
    def step(tokens, gate_weight, up_weight, down_weight):
        c = CHUNKS
        shapes = [
            ((KB, 2 * FB), BF),
            ((FB, KB), BF),
            ((c, 2, 2, 2, ROWS, KB), BF),
            ((c, 4, 2, ROWS, 2 * FB), BF),
            ((c, 4, 2, ROWS, 2 * FB), F32),
            ((c, 2, ROWS, FB), BF),
            ((c, 2, ROWS, FB), BF),
            ((c, 2, 2, ROWS, FB), BF),
            ((c, ROWS, FB), BF),
            ((c, ROWS, FB), BF),
            ((c, 4, ROWS, FB), BF),
            ((c, 4, ROWS, FB), BF),
            ((c, 4, ROWS, FB), F32),
            ((c, ROWS, FB), BF),
            ((c, ROWS, FB), BF),
            ((c, 2, ROWS, FB), BF),
            ((c, 4, 2, ROWS, FB), BF),
            ((c, 4, 2, ROWS, KB), F32),
            ((c, 4, ROWS, KB), F32),
            ((c, 4, ROWS, KB), BF),
            ((c, 4, ROWS, KB), BF),
            ((ROWS, KB), F32),
        ]
        return pl.pallas_call(
            kernel,
            name="swiglu",
            out_shape=jax.ShapeDtypeStruct((ROWS, KB), BF),
            in_specs=[pl.BlockSpec(memory_space=pl.ANY)] * 4,
            out_specs=pl.BlockSpec(memory_space=pltpu.VMEM),
            scratch_shapes=[pltpu.VMEM(s, d) for s, d in shapes]
            + [pltpu.SemaphoreType.DMA((N_SEM,)), pltpu.SemaphoreType.DMA((N_SEM,)), pltpu.SemaphoreType.DMA((4,))],
            compiler_params=pltpu.CompilerParams(collective_id=0, has_side_effects=True, vmem_limit_bytes=60 * 2**20),
        )(tokens, gate_weight, up_weight, down_weight)

    return jax.shard_map(
        step,
        mesh=mesh,
        in_specs=(
            P(("inp", "out"), "wt"),
            P("wt", ("inp", "out")),
            P("wt", ("inp", "out")),
            P(("inp", "out"), "wt"),
        ),
        out_specs=P(("inp", "out"), "wt"),
        check_vma=False,
    )
```

```python
import jax
import jax.numpy as jnp
from jax import lax
from jax.experimental import pallas as pl
from jax.experimental.pallas import tpu as pltpu
from jax.sharding import PartitionSpec as P

MESH = pl.DeviceIdType.MESH
BF, F32 = jnp.bfloat16, jnp.float32

ROWS = 48
KB = 1024
FB = 896
HALF = 512
CHUNKS = 4
OFFS = ((0, -1), (2, -2), (3, 4), (1, -3))
SLOT = {o: (c, zi) for c, pair in enumerate(OFFS) for zi, o in enumerate(pair)}
STAGES = ("xr", "m1", "s2", "s3", "s4", "a2", "a3", "m2", "g1")
ORDER = (
    2, 3, 4, 10, 5, 6, 11, 7, 20, 9, 13, 12, 21, 23, 31, 33, 22, 41, 32, 51, 43, 61, 30, 53,
    42, 71, 63, 52, 40, 81, 73, 62, 83, 72, 50, 82, 60, 70, 80,
)
N_SEM = 192


def kernel(tok, wg, wu, wd, out, w1, w2, x, p16, p32, gr1, sb, gr2, gs, gx, ux, q16, q32, ur1, uv, ur2, h, o32, cr, zs, zr, own,
           ssem, rsem, lsem):
    z = lax.axis_index("inp")
    wt = lax.axis_index("wt")
    ot = lax.axis_index("out")
    a, y = wt // 4, wt % 4
    xh, core = ot // 2, ot % 2
    na = 1 - a
    yr, yl, yo = (y + 1) % 4, (y + 3) % 4, (y + 2) % 4

    def dev(dz=0, dx=0, dc=0):
        return (lax.rem(z + dz + 8, 8), wt, (xh + dx) % 2 * 2 + (core + dc) % 2)

    sibling = dev(dc=1)
    right, left, across = (z, a * 4 + yr, ot), (z, a * 4 + yl, ot), (z, na * 4 + y, ot)

    loads = [
        pltpu.make_async_copy(tok, x.at[SLOT[0] + (0, 0)], lsem.at[0]),
        pltpu.make_async_copy(wg, w1.at[:, pl.ds(0, FB)], lsem.at[1]),
        pltpu.make_async_copy(wu, w1.at[:, pl.ds(FB, FB)], lsem.at[2]),
        pltpu.make_async_copy(wd, w2, lsem.at[3]),
    ]
    for load in loads:
        load.start()

    barrier = pltpu.get_barrier_semaphore()
    peers = [sibling, right, left, across, dev(dx=1), dev(dz=1), dev(dz=-1)]
    for peer in peers:
        pl.semaphore_signal(barrier, inc=1, device_id=peer, device_id_type=MESH)
    pl.semaphore_wait(barrier, len(peers))

    copies = {}

    def send(name, src, dst, to):
        i = len(copies)
        cp = pltpu.make_async_remote_copy(
            src_ref=src, dst_ref=dst, send_sem=ssem.at[i], recv_sem=rsem.at[i], device_id=to, device_id_type=MESH
        )
        cp.start()
        copies[name] = cp

    def got(*names):
        for name in names:
            copies[name].wait_recv()

    def xs(o, rx, rc):
        return x.at[SLOT[o] + (rx, rc)]

    def hop(k, rx, step):
        o = k - step
        o = 4 if o == -4 else o
        send(("x", o, rx), xs(k, rx, 0), xs(o, rx, 0), dev(dz=step))

    loads[0].wait()
    hop(0, 0, 1)
    hop(0, 0, -1)
    send("x_hi", xs(0, 0, 0), xs(0, 1, 0), dev(dx=1))
    send("x_c0", xs(0, 0, 0), xs(0, 0, 1), sibling)
    got("x_hi")
    hop(0, 1, 1)
    hop(0, 1, -1)
    send("x_c1", xs(0, 1, 0), xs(0, 1, 1), sibling)

    def to_sibling(o):
        c, zi = SLOT[o]
        send(("xc", o), x.at[c, zi, :, 0], x.at[c, zi, :, 1], sibling)

    def xr(k):
        k, rx = k // 2, k % 2
        if k == 4:
            got(("x", 4, 0), ("x", 4, 1))
            to_sibling(4)
            return
        got(("x", -k, rx))
        if k < 3 or rx == 0:
            hop(-k, rx, 1)
        got(("x", k, rx))
        if k < 3 or rx == 1:
            hop(k, rx, -1)
        if rx == 1:
            to_sibling(k)
            to_sibling(-k)

    waited = set()

    def once(*which):
        for i in which:
            if i not in waited:
                waited.add(i)
                loads[i].wait()

    def m1(c):
        once(1, 2)
        for o in OFFS[c]:
            if o:
                got(("xc", o))
            else:
                got("x_c0", "x_c1")

        def tile(j, _):
            cols = pl.ds(pl.multiple_of(j * 256, 256), 256)
            r = jnp.dot(x[c].reshape(8 * ROWS, KB), w1[:, cols], preferred_element_type=F32)
            r = r.reshape(4, 2, ROWS, 256)
            p32[c, :, :, :, cols] = r
            p16[c, :, :, :, cols] = r.astype(BF)
            return 0

        lax.fori_loop(0, 7, tile, 0)
        g, u = pl.ds(0, FB), pl.ds(FB, FB)
        send(("u0", c), p16.at[c, :, na, :, u], ux.at[c], across)
        send(("g1r", c), p16.at[c, yo, 0, :, g], gr1.at[c, 0], right)
        send(("g1l", c), p16.at[c, yo, 1, :, g], gr1.at[c, 1], left)
        send(("g2r1", c), p16.at[c, yr, 1, :, g], gr2.at[c, 0, 1], right)
        send(("g2l0", c), p16.at[c, yl, 0, :, g], gr2.at[c, 1, 0], left)

    def s2(c):
        got(("g1r", c))
        sb[c, 0] = (p32[c, yr, 0, :, :FB] + gr1[c, 0].astype(F32)).astype(BF)
        send(("g2r0", c), sb.at[c, 0], gr2.at[c, 0, 0], right)
        got(("g1l", c))
        sb[c, 1] = (p32[c, yl, 1, :, :FB] + gr1[c, 1].astype(F32)).astype(BF)
        send(("g2l1", c), sb.at[c, 1], gr2.at[c, 1, 1], left)
        got(("u0", c))
        for k in range(4):
            q = p32[c, k, a, :, FB:] + ux[c, k].astype(F32)
            q32[c, k] = q
            q16[c, k] = q.astype(BF)
        lo, hi = pl.ds(0, HALF), pl.ds(HALF, FB - HALF)
        send(("u1r", c), q16.at[c, yo, :, lo], ur1.at[c, :, lo], right)
        send(("u1l", c), q16.at[c, yo, :, hi], ur1.at[c, :, hi], left)
        send(("u2rh", c), q16.at[c, yr, :, hi], ur2.at[c, 0, :, hi], right)
        send(("u2ll", c), q16.at[c, yl, :, lo], ur2.at[c, 1, :, lo], left)

    def s3(c):
        got(("g2r0", c), ("g2r1", c), ("g2l0", c), ("g2l1", c))
        t = p32[c, y, na, :, :FB] + gr2[c, 0, na].astype(F32) + gr2[c, 1, na].astype(F32)
        gs[c] = t.astype(BF)
        send(("gx", c), gs.at[c], gx.at[c], across)
        lo, hi = pl.ds(0, HALF), pl.ds(HALF, FB - HALF)
        got(("u1r", c))
        uv[c, :, :HALF] = (q32[c, yr, :, :HALF] + ur1[c, :, :HALF].astype(F32)).astype(BF)
        send(("u2rl", c), uv.at[c, :, lo], ur2.at[c, 0, :, lo], right)
        got(("u1l", c))
        uv[c, :, HALF:] = (q32[c, yl, :, HALF:] + ur1[c, :, HALF:].astype(F32)).astype(BF)
        send(("u2lh", c), uv.at[c, :, hi], ur2.at[c, 1, :, hi], left)

    def s4(c):
        got(("gx", c), ("u2rl", c), ("u2rh", c), ("u2ll", c), ("u2lh", c))
        gate = p32[c, y, a, :, :FB] + gr2[c, 0, a].astype(F32) + gr2[c, 1, a].astype(F32) + gx[c].astype(F32)
        up = q32[c, y] + ur2[c, 0].astype(F32) + ur2[c, 1].astype(F32)
        h[c, y, a] = (gate * jax.nn.sigmoid(gate) * up).astype(BF)
        send(("hx", c), h.at[c, y, a], h.at[c, y, a], across)
        send(("hr", c), h.at[c, y, a], h.at[c, y, a], right)
        send(("hl", c), h.at[c, y, a], h.at[c, y, a], left)

    def a2(c):
        got(("hx", c))
        send(("pr", c), h.at[c, y, na], h.at[c, y, na], right)
        send(("pl", c), h.at[c, y, na], h.at[c, y, na], left)

    def a3(c):
        got(("hr", c))
        send(("fr", c), h.at[c, yl, a], h.at[c, yl, a], right)
        got(("pl", c))
        send(("fl", c), h.at[c, yr, na], h.at[c, yr, na], left)

    def m2(c):
        once(3)
        got(("hl", c), ("pr", c), ("fr", c), ("fl", c))

        def tile(j, _):
            cols = pl.ds(pl.multiple_of(j * 256, 256), 256)
            r = jnp.dot(h[c].reshape(8 * ROWS, FB), w2[:, cols], preferred_element_type=F32)
            o32[c, :, :, :, cols] = r.reshape(4, 2, ROWS, 256)
            return 0

        lax.fori_loop(0, 4, tile, 0)
        send(("c", c), o32.at[c, :, 1], cr.at[c], sibling)

    def g1(c):
        got(("c", c))
        for zi in range(2):
            for dx in range(2):
                k = zi * 2 + dx
                v = o32[c, k, 0] + cr[c, k]
                if OFFS[c][zi] == 0 and dx == 0:
                    own[...] = v
                else:
                    zs[c, k] = v.astype(BF)
                    send(("z", c, k), zs.at[c, k], zr.at[c, k], dev(dz=OFFS[c][zi], dx=dx))

    stages = dict(xr=xr, m1=m1, s2=s2, s3=s3, s4=s4, a2=a2, a3=a3, m2=m2, g1=g1)
    for i in ORDER:
        s, c = STAGES[i // 10], i % 10
        with jax.named_scope(f"{s}_{c}"):
            stages[s](c)

    total = own[...]
    for c in range(CHUNKS):
        for k in range(4):
            if ("z", c, k) in copies:
                got(("z", c, k))
                total += zr[c, k].astype(F32)
    out[...] = total.astype(BF)
    for cp in copies.values():
        cp.wait_send()


def solution(mesh):
    def step(tokens, gate_weight, up_weight, down_weight):
        c = CHUNKS
        shapes = [
            ((KB, 2 * FB), BF),
            ((FB, KB), BF),
            ((c, 2, 2, 2, ROWS, KB), BF),
            ((c, 4, 2, ROWS, 2 * FB), BF),
            ((c, 4, 2, ROWS, 2 * FB), F32),
            ((c, 2, ROWS, FB), BF),
            ((c, 2, ROWS, FB), BF),
            ((c, 2, 2, ROWS, FB), BF),
            ((c, ROWS, FB), BF),
            ((c, ROWS, FB), BF),
            ((c, 4, ROWS, FB), BF),
            ((c, 4, ROWS, FB), BF),
            ((c, 4, ROWS, FB), F32),
            ((c, ROWS, FB), BF),
            ((c, ROWS, FB), BF),
            ((c, 2, ROWS, FB), BF),
            ((c, 4, 2, ROWS, FB), BF),
            ((c, 4, 2, ROWS, KB), F32),
            ((c, 4, ROWS, KB), F32),
            ((c, 4, ROWS, KB), BF),
            ((c, 4, ROWS, KB), BF),
            ((ROWS, KB), F32),
        ]
        return pl.pallas_call(
            kernel,
            name="swiglu",
            out_shape=jax.ShapeDtypeStruct((ROWS, KB), BF),
            in_specs=[pl.BlockSpec(memory_space=pl.ANY)] * 4,
            out_specs=pl.BlockSpec(memory_space=pltpu.VMEM),
            scratch_shapes=[pltpu.VMEM(s, d) for s, d in shapes]
            + [pltpu.SemaphoreType.DMA((N_SEM,)), pltpu.SemaphoreType.DMA((N_SEM,)), pltpu.SemaphoreType.DMA((4,))],
            compiler_params=pltpu.CompilerParams(collective_id=0, has_side_effects=True, vmem_limit_bytes=60 * 2**20),
        )(tokens, gate_weight, up_weight, down_weight)

    return jax.shard_map(
        step,
        mesh=mesh,
        in_specs=(
            P(("inp", "out"), "wt"),
            P("wt", ("inp", "out")),
            P("wt", ("inp", "out")),
            P(("inp", "out"), "wt"),
        ),
        out_specs=P(("inp", "out"), "wt"),
        check_vma=False,
    )
```

```python
import jax
import jax.numpy as jnp
from jax import lax
from jax.experimental import pallas as pl
from jax.experimental.pallas import tpu as pltpu
from jax.sharding import PartitionSpec as P

MESH = pl.DeviceIdType.MESH
BF, F32 = jnp.bfloat16, jnp.float32

ROWS = 48
KB = 1024
FB = 896
HID = ((0, 512), (512, 384))
COL = ((0, 1024), (1024, 768))
YF = ((0, 640), (640, 384))
XF = ((0, 384), (384, 384))
YW, XW = 1024, 768
LO = 256
CHUNKS = 4
OFFS = ((0, -1), (2, -2), (3, 4), (1, -3))
SLOT = {o: (c, zi) for c, pair in enumerate(OFFS) for zi, o in enumerate(pair)}
STAGES = ("xr", "m1", "s2", "s3", "s4", "a2", "a3", "m2", "g1")
ORDER = (
    2, 3, 4, 10, 5, 11, 6, 12, 7, 13, 20, 21, 9, 22, 15, 14, 23, 32, 25, 16, 33, 42, 24, 17,
    52, 43, 34, 35, 31, 53, 30, 62, 44, 63, 45, 26, 54, 55, 27, 71, 40, 64, 65, 41, 36, 37, 81, 51,
    50, 72, 47, 46, 60, 61, 82, 57, 56, 70, 67, 66, 80, 73, 83,
)
N_SEM = 240


def kernel(tok, wg, wu, wd, out, w1, w2, x, p16, p32, gr1, sb, gr2, gs, gx, ux, q16, q32, ur1, uv, ur2, h, o32, cr, zs, zr, own,
           ssem, rsem, lsem):
    z = lax.axis_index("inp")
    wt = lax.axis_index("wt")
    ot = lax.axis_index("out")
    a, y = wt // 4, wt % 4
    xh, core = ot // 2, ot % 2
    na = 1 - a
    yr, yl, yo = (y + 1) % 4, (y + 3) % 4, (y + 2) % 4

    def dev(dz=0, dx=0, dc=0):
        return (lax.rem(z + dz + 8, 8), wt, (xh + dx) % 2 * 2 + (core + dc) % 2)

    sibling = dev(dc=1)
    right, left, across = (z, a * 4 + yr, ot), (z, a * 4 + yl, ot), (z, na * 4 + y, ot)

    loads = [
        pltpu.make_async_copy(tok, x.at[SLOT[0] + (0, 0)], lsem.at[0]),
        pltpu.make_async_copy(wd, w2, lsem.at[1]),
    ]
    for p in range(2):
        (at, n), col = HID[p], COL[p][0]
        loads.append(pltpu.make_async_copy(wg.at[:, pl.ds(at, n)], w1.at[:, pl.ds(col, n)], lsem.at[2 + 2 * p]))
        loads.append(pltpu.make_async_copy(wu.at[:, pl.ds(at, n)], w1.at[:, pl.ds(col + n, n)], lsem.at[3 + 2 * p]))
    for load in loads:
        load.start()

    barrier = pltpu.get_barrier_semaphore()
    peers = [sibling, right, left, across, dev(dx=1), dev(dz=1), dev(dz=-1)]
    for peer in peers:
        pl.semaphore_signal(barrier, inc=1, device_id=peer, device_id_type=MESH)
    pl.semaphore_wait(barrier, len(peers))

    copies = {}

    def send(name, src, dst, to):
        i = len(copies)
        cp = pltpu.make_async_remote_copy(
            src_ref=src, dst_ref=dst, send_sem=ssem.at[i], recv_sem=rsem.at[i], device_id=to, device_id_type=MESH
        )
        cp.start()
        copies[name] = cp

    def got(*names):
        for name in names:
            copies[name].wait_recv()

    def xs(o, rx, rc):
        return x.at[SLOT[o] + (rx, rc)]

    def hop(k, rx, step):
        o = k - step
        o = 4 if o == -4 else o
        send(("x", o, rx), xs(k, rx, 0), xs(o, rx, 0), dev(dz=step))

    loads[0].wait()
    hop(0, 0, 1)
    hop(0, 0, -1)
    send("x_hi", xs(0, 0, 0), xs(0, 1, 0), dev(dx=1))
    send("x_c0", xs(0, 0, 0), xs(0, 0, 1), sibling)
    got("x_hi")
    hop(0, 1, 1)
    hop(0, 1, -1)
    send("x_c1", xs(0, 1, 0), xs(0, 1, 1), sibling)

    def to_sibling(o):
        c, zi = SLOT[o]
        send(("xc", o), x.at[c, zi, :, 0], x.at[c, zi, :, 1], sibling)

    def xr(k):
        k, rx = k // 2, k % 2
        if k == 4:
            got(("x", 4, 0), ("x", 4, 1))
            to_sibling(4)
            return
        got(("x", -k, rx))
        if k < 3 or rx == 0:
            hop(-k, rx, 1)
        got(("x", k, rx))
        if k < 3 or rx == 1:
            hop(k, rx, -1)
        if rx == 1:
            to_sibling(k)
            to_sibling(-k)

    waited = set()

    def once(*which):
        for i in which:
            if i not in waited:
                waited.add(i)
                loads[i].wait()

    def yf(i, at=0, n=None):
        return pl.ds(YF[i % 2][0] + at, YF[i % 2][1] - at if n is None else n)

    def xf(i, at=0, n=None):
        return pl.ds(XF[i % 2][0] + at, XF[i % 2][1] - at if n is None else n)

    def pcols(i):
        col, width = COL[i % 2]
        n = YF[i % 2][1]
        return pl.ds(col, n), pl.ds(col + n, width - n)

    def hid(i):
        return pl.ds(*HID[i % 2])

    def m1(i):
        c, p = i // 2, i % 2
        once(2 + 2 * p, 3 + 2 * p)
        for o in OFFS[c]:
            if ("xo", o) not in waited:
                waited.add(("xo", o))
                if o:
                    got(("xc", o))
                else:
                    got("x_c0", "x_c1")

        def tile(j, _):
            cols = pl.ds(pl.multiple_of(COL[p][0] + j * 256, 256), 256)
            r = jnp.dot(x[c].reshape(8 * ROWS, KB), w1[:, cols], preferred_element_type=F32)
            r = r.reshape(4, 2, ROWS, 256)
            p32[c, :, :, :, cols] = r
            p16[c, :, :, :, cols] = r.astype(BF)
            return 0

        lax.fori_loop(0, COL[p][1] // 256, tile, 0)
        g, u = pcols(i)
        send(("u0", i), p16.at[c, :, na, :, u], ux.at[c, :, :, xf(i)], across)
        send(("g1r", i), p16.at[c, yo, 0, :, g], gr1.at[c, 0, :, yf(i)], right)
        send(("g1l", i), p16.at[c, yo, 1, :, g], gr1.at[c, 1, :, yf(i)], left)
        send(("g2r1", i), p16.at[c, yr, 1, :, g], gr2.at[c, 0, 1, :, yf(i)], right)
        send(("g2l0", i), p16.at[c, yl, 0, :, g], gr2.at[c, 1, 0, :, yf(i)], left)

    def s2(i):
        c = i // 2
        g, u = pcols(i)
        f, v = yf(i), xf(i)
        got(("g1r", i))
        sb[c, 0, :, f] = (p32[c, yr, 0, :, g] + gr1[c, 0, :, f].astype(F32)).astype(BF)
        send(("g2r0", i), sb.at[c, 0, :, f], gr2.at[c, 0, 0, :, f], right)
        got(("g1l", i))
        sb[c, 1, :, f] = (p32[c, yl, 1, :, g] + gr1[c, 1, :, f].astype(F32)).astype(BF)
        send(("g2l1", i), sb.at[c, 1, :, f], gr2.at[c, 1, 1, :, f], left)
        got(("u0", i))
        for k in range(4):
            q = p32[c, k, a, :, u] + ux[c, k, :, v].astype(F32)
            q32[c, k, :, v] = q
            q16[c, k, :, v] = q.astype(BF)
        lo, hi = xf(i, 0, LO), xf(i, LO)
        send(("u1r", i), q16.at[c, yo, :, lo], ur1.at[c, :, lo], right)
        send(("u1l", i), q16.at[c, yo, :, hi], ur1.at[c, :, hi], left)
        send(("u2rh", i), q16.at[c, yr, :, hi], ur2.at[c, 0, :, hi], right)
        send(("u2ll", i), q16.at[c, yl, :, lo], ur2.at[c, 1, :, lo], left)

    def s3(i):
        c = i // 2
        g, _ = pcols(i)
        f = yf(i)
        got(("g2r0", i), ("g2r1", i), ("g2l0", i), ("g2l1", i))
        t = p32[c, y, na, :, g] + gr2[c, 0, na, :, f].astype(F32) + gr2[c, 1, na, :, f].astype(F32)
        gs[c, :, f] = t.astype(BF)
        send(("gx", i), gs.at[c, :, f], gx.at[c, :, f], across)
        lo, hi = xf(i, 0, LO), xf(i, LO)
        got(("u1r", i))
        uv[c, :, lo] = (q32[c, yr, :, lo] + ur1[c, :, lo].astype(F32)).astype(BF)
        send(("u2rl", i), uv.at[c, :, lo], ur2.at[c, 0, :, lo], right)
        got(("u1l", i))
        uv[c, :, hi] = (q32[c, yl, :, hi] + ur1[c, :, hi].astype(F32)).astype(BF)
        send(("u2lh", i), uv.at[c, :, hi], ur2.at[c, 1, :, hi], left)

    def s4(i):
        c = i // 2
        g, _ = pcols(i)
        f, v, e = yf(i), xf(i), hid(i)
        n = HID[i % 2][1]
        got(("gx", i), ("u2rl", i), ("u2rh", i), ("u2ll", i), ("u2lh", i))
        t = p32[c, y, a, :, g] + gr2[c, 0, a, :, f].astype(F32) + gr2[c, 1, a, :, f].astype(F32) + gx[c, :, f].astype(F32)
        up = q32[c, y, :, v] + ur2[c, 0, :, v].astype(F32) + ur2[c, 1, :, v].astype(F32)
        gate = t[:, :n]
        if YF[i % 2][1] > n:
            up = jnp.concatenate([t[:, n:], up], axis=1)
        h[c, y, a, :, e] = (gate * jax.nn.sigmoid(gate) * up).astype(BF)
        own_h = h.at[c, y, a, :, e]
        send(("hx", i), own_h, own_h, across)
        send(("hr", i), own_h, own_h, right)
        send(("hl", i), own_h, own_h, left)

    def a2(i):
        got(("hx", i))
        block = h.at[i // 2, y, na, :, hid(i)]
        send(("pr", i), block, block, right)
        send(("pl", i), block, block, left)

    def a3(i):
        got(("hr", i))
        block = h.at[i // 2, yl, a, :, hid(i)]
        send(("fr", i), block, block, right)
        got(("pl", i))
        block = h.at[i // 2, yr, na, :, hid(i)]
        send(("fl", i), block, block, left)

    def m2(c):
        once(1)
        for i in (2 * c, 2 * c + 1):
            got(("hl", i), ("pr", i), ("fr", i), ("fl", i))

        def tile(j, _):
            cols = pl.ds(pl.multiple_of(j * 256, 256), 256)
            r = jnp.dot(h[c].reshape(8 * ROWS, FB), w2[:, cols], preferred_element_type=F32)
            o32[c, :, :, :, cols] = r.reshape(4, 2, ROWS, 256)
            return 0

        lax.fori_loop(0, 4, tile, 0)
        send(("c", c), o32.at[c, :, 1], cr.at[c], sibling)

    def g1(c):
        got(("c", c))
        for zi in range(2):
            for dx in range(2):
                k = zi * 2 + dx
                v = o32[c, k, 0] + cr[c, k]
                if OFFS[c][zi] == 0 and dx == 0:
                    own[...] = v
                else:
                    zs[c, k] = v.astype(BF)
                    send(("z", c, k), zs.at[c, k], zr.at[c, k], dev(dz=OFFS[c][zi], dx=dx))

    stages = dict(xr=xr, m1=m1, s2=s2, s3=s3, s4=s4, a2=a2, a3=a3, m2=m2, g1=g1)
    for i in ORDER:
        s, c = STAGES[i // 10], i % 10
        with jax.named_scope(f"{s}_{c}"):
            stages[s](c)

    total = own[...]
    for c in range(CHUNKS):
        for k in range(4):
            if ("z", c, k) in copies:
                got(("z", c, k))
                total += zr[c, k].astype(F32)
    out[...] = total.astype(BF)
    for cp in copies.values():
        cp.wait_send()


def solution(mesh):
    def step(tokens, gate_weight, up_weight, down_weight):
        c = CHUNKS
        shapes = [
            ((KB, 2 * FB), BF),
            ((FB, KB), BF),
            ((c, 2, 2, 2, ROWS, KB), BF),
            ((c, 4, 2, ROWS, 2 * FB), BF),
            ((c, 4, 2, ROWS, 2 * FB), F32),
            ((c, 2, ROWS, YW), BF),
            ((c, 2, ROWS, YW), BF),
            ((c, 2, 2, ROWS, YW), BF),
            ((c, ROWS, YW), BF),
            ((c, ROWS, YW), BF),
            ((c, 4, ROWS, XW), BF),
            ((c, 4, ROWS, XW), BF),
            ((c, 4, ROWS, XW), F32),
            ((c, ROWS, XW), BF),
            ((c, ROWS, XW), BF),
            ((c, 2, ROWS, XW), BF),
            ((c, 4, 2, ROWS, FB), BF),
            ((c, 4, 2, ROWS, KB), F32),
            ((c, 4, ROWS, KB), F32),
            ((c, 4, ROWS, KB), BF),
            ((c, 4, ROWS, KB), BF),
            ((ROWS, KB), F32),
        ]
        return pl.pallas_call(
            kernel,
            name="swiglu",
            out_shape=jax.ShapeDtypeStruct((ROWS, KB), BF),
            in_specs=[pl.BlockSpec(memory_space=pl.ANY)] * 4,
            out_specs=pl.BlockSpec(memory_space=pltpu.VMEM),
            scratch_shapes=[pltpu.VMEM(s, d) for s, d in shapes]
            + [pltpu.SemaphoreType.DMA((N_SEM,)), pltpu.SemaphoreType.DMA((N_SEM,)), pltpu.SemaphoreType.DMA((6,))],
            compiler_params=pltpu.CompilerParams(collective_id=0, has_side_effects=True, vmem_limit_bytes=60 * 2**20),
        )(tokens, gate_weight, up_weight, down_weight)

    return jax.shard_map(
        step,
        mesh=mesh,
        in_specs=(
            P(("inp", "out"), "wt"),
            P("wt", ("inp", "out")),
            P("wt", ("inp", "out")),
            P(("inp", "out"), "wt"),
        ),
        out_specs=P(("inp", "out"), "wt"),
        check_vma=False,
    )
```

```python
import jax
import jax.numpy as jnp
from jax import lax
from jax.experimental import pallas as pl
from jax.experimental.pallas import tpu as pltpu
from jax.sharding import PartitionSpec as P

MESH = pl.DeviceIdType.MESH
BF, F32 = jnp.bfloat16, jnp.float32

ROWS = 48
KB = 1024
FB = 896
HID = ((0, 512), (512, 384))
COL = ((0, 1024), (1024, 768))
YF = ((0, 640), (640, 384))
XF = ((0, 384), (384, 384))
YW, XW = 1024, 768
LO = 256
CHUNKS = 4
WIDE = (1, -1)
OFFS = ((1, -1), (3, -3), (2, 4), (0, -2))
SLOT = {o: (c, zi) for c, pair in enumerate(OFFS) for zi, o in enumerate(pair)}
STAGES = ("xr", "m1", "s2", "s3", "s4", "a2", "a3", "m2", "g1", "g2")
ORDER = (
    2, 3, 4, 11, 5, 10, 6, 17, 21, 7, 16, 20, 13, 9, 12, 26, 31, 30, 14, 15, 41, 23, 40, 27,
    22, 25, 37, 33, 51, 32, 24, 36, 43, 50, 42, 35, 53, 52, 34, 60, 61, 47, 63, 46, 62, 45, 44, 70,
    55, 54, 57, 56, 71, 80, 65, 64, 66, 81, 67, 72, 90, 73, 82, 91, 83, 92, 93,
)
N_SEM = 240


def kernel(tok, wg, wu, wd, out, w1, w2, x, p16, p32, gr1, sb, gr2, gs, gx, ux, q16, q32, ur1, uv, ur2, h, o32, cr, zs, zr, own, ws, wr,
           ssem, rsem, lsem):
    z = lax.axis_index("inp")
    wt = lax.axis_index("wt")
    ot = lax.axis_index("out")
    a, y = wt // 4, wt % 4
    xh, core = ot // 2, ot % 2
    na = 1 - a
    yr, yl, yo = (y + 1) % 4, (y + 3) % 4, (y + 2) % 4

    def dev(dz=0, dx=0, dc=0):
        return (lax.rem(z + dz + 8, 8), wt, (xh + dx) % 2 * 2 + (core + dc) % 2)

    sibling = dev(dc=1)
    right, left, across = (z, a * 4 + yr, ot), (z, a * 4 + yl, ot), (z, na * 4 + y, ot)

    loads = [
        pltpu.make_async_copy(tok, x.at[SLOT[0] + (0, 0)], lsem.at[0]),
        pltpu.make_async_copy(wd, w2, lsem.at[1]),
    ]
    for p in range(2):
        (at, n), col = HID[p], COL[p][0]
        loads.append(pltpu.make_async_copy(wg.at[:, pl.ds(at, n)], w1.at[:, pl.ds(col, n)], lsem.at[2 + 2 * p]))
        loads.append(pltpu.make_async_copy(wu.at[:, pl.ds(at, n)], w1.at[:, pl.ds(col + n, n)], lsem.at[3 + 2 * p]))
    for load in loads:
        load.start()

    barrier = pltpu.get_barrier_semaphore()
    peers = [sibling, right, left, across, dev(dx=1), dev(dz=1), dev(dz=-1)]
    for peer in peers:
        pl.semaphore_signal(barrier, inc=1, device_id=peer, device_id_type=MESH)
    pl.semaphore_wait(barrier, len(peers))

    copies = {}

    def send(name, src, dst, to):
        i = len(copies)
        cp = pltpu.make_async_remote_copy(
            src_ref=src, dst_ref=dst, send_sem=ssem.at[i], recv_sem=rsem.at[i], device_id=to, device_id_type=MESH
        )
        cp.start()
        copies[name] = cp

    def got(*names):
        for name in names:
            copies[name].wait_recv()

    def xs(o, rx, rc):
        return x.at[SLOT[o] + (rx, rc)]

    def hop(k, rx, step):
        o = k - step
        o = 4 if o == -4 else o
        send(("x", o, rx), xs(k, rx, 0), xs(o, rx, 0), dev(dz=step))

    loads[0].wait()
    hop(0, 0, 1)
    hop(0, 0, -1)
    send("x_hi", xs(0, 0, 0), xs(0, 1, 0), dev(dx=1))
    send("x_c0", xs(0, 0, 0), xs(0, 0, 1), sibling)
    got("x_hi")
    hop(0, 1, 1)
    hop(0, 1, -1)
    send("x_c1", xs(0, 1, 0), xs(0, 1, 1), sibling)

    def to_sibling(o):
        c, zi = SLOT[o]
        send(("xc", o), x.at[c, zi, :, 0], x.at[c, zi, :, 1], sibling)

    def xr(k):
        k, rx = k // 2, k % 2
        if k == 4:
            got(("x", 4, 0), ("x", 4, 1))
            to_sibling(4)
            return
        got(("x", -k, rx))
        if k < 3 or rx == 0:
            hop(-k, rx, 1)
        got(("x", k, rx))
        if k < 3 or rx == 1:
            hop(k, rx, -1)
        if rx == 1:
            to_sibling(k)
            to_sibling(-k)

    waited = set()

    def once(*which):
        for i in which:
            if i not in waited:
                waited.add(i)
                loads[i].wait()

    def yf(i, at=0, n=None):
        return pl.ds(YF[i % 2][0] + at, YF[i % 2][1] - at if n is None else n)

    def xf(i, at=0, n=None):
        return pl.ds(XF[i % 2][0] + at, XF[i % 2][1] - at if n is None else n)

    def pcols(i):
        col, width = COL[i % 2]
        n = YF[i % 2][1]
        return pl.ds(col, n), pl.ds(col + n, width - n)

    def hid(i):
        return pl.ds(*HID[i % 2])

    def m1(i):
        c, p = i // 2, i % 2
        once(2 + 2 * p, 3 + 2 * p)
        for o in OFFS[c]:
            if ("xo", o) not in waited:
                waited.add(("xo", o))
                if o:
                    got(("xc", o))
                else:
                    got("x_c0", "x_c1")

        def tile(j, _):
            cols = pl.ds(pl.multiple_of(COL[p][0] + j * 256, 256), 256)
            r = jnp.dot(x[c].reshape(8 * ROWS, KB), w1[:, cols], preferred_element_type=F32)
            r = r.reshape(4, 2, ROWS, 256)
            p32[c, :, :, :, cols] = r
            p16[c, :, :, :, cols] = r.astype(BF)
            return 0

        lax.fori_loop(0, COL[p][1] // 256, tile, 0)
        g, u = pcols(i)
        send(("u0", i), p16.at[c, :, na, :, u], ux.at[c, :, :, xf(i)], across)
        send(("g1r", i), p16.at[c, yo, 0, :, g], gr1.at[c, 0, :, yf(i)], right)
        send(("g1l", i), p16.at[c, yo, 1, :, g], gr1.at[c, 1, :, yf(i)], left)
        send(("g2r1", i), p16.at[c, yr, 1, :, g], gr2.at[c, 0, 1, :, yf(i)], right)
        send(("g2l0", i), p16.at[c, yl, 0, :, g], gr2.at[c, 1, 0, :, yf(i)], left)

    def s2(i):
        c = i // 2
        g, u = pcols(i)
        f, v = yf(i), xf(i)
        got(("g1r", i))
        sb[c, 0, :, f] = (p32[c, yr, 0, :, g] + gr1[c, 0, :, f].astype(F32)).astype(BF)
        send(("g2r0", i), sb.at[c, 0, :, f], gr2.at[c, 0, 0, :, f], right)
        got(("g1l", i))
        sb[c, 1, :, f] = (p32[c, yl, 1, :, g] + gr1[c, 1, :, f].astype(F32)).astype(BF)
        send(("g2l1", i), sb.at[c, 1, :, f], gr2.at[c, 1, 1, :, f], left)
        got(("u0", i))
        for k in range(4):
            q = p32[c, k, a, :, u] + ux[c, k, :, v].astype(F32)
            q32[c, k, :, v] = q
            q16[c, k, :, v] = q.astype(BF)
        lo, hi = xf(i, 0, LO), xf(i, LO)
        send(("u1r", i), q16.at[c, yo, :, lo], ur1.at[c, :, lo], right)
        send(("u1l", i), q16.at[c, yo, :, hi], ur1.at[c, :, hi], left)
        send(("u2rh", i), q16.at[c, yr, :, hi], ur2.at[c, 0, :, hi], right)
        send(("u2ll", i), q16.at[c, yl, :, lo], ur2.at[c, 1, :, lo], left)

    def s3(i):
        c = i // 2
        g, _ = pcols(i)
        f = yf(i)
        got(("g2r0", i), ("g2r1", i), ("g2l0", i), ("g2l1", i))
        t = p32[c, y, na, :, g] + gr2[c, 0, na, :, f].astype(F32) + gr2[c, 1, na, :, f].astype(F32)
        gs[c, :, f] = t.astype(BF)
        send(("gx", i), gs.at[c, :, f], gx.at[c, :, f], across)
        lo, hi = xf(i, 0, LO), xf(i, LO)
        got(("u1r", i))
        uv[c, :, lo] = (q32[c, yr, :, lo] + ur1[c, :, lo].astype(F32)).astype(BF)
        send(("u2rl", i), uv.at[c, :, lo], ur2.at[c, 0, :, lo], right)
        got(("u1l", i))
        uv[c, :, hi] = (q32[c, yl, :, hi] + ur1[c, :, hi].astype(F32)).astype(BF)
        send(("u2lh", i), uv.at[c, :, hi], ur2.at[c, 1, :, hi], left)

    def s4(i):
        c = i // 2
        g, _ = pcols(i)
        f, v, e = yf(i), xf(i), hid(i)
        n = HID[i % 2][1]
        got(("gx", i), ("u2rl", i), ("u2rh", i), ("u2ll", i), ("u2lh", i))
        t = p32[c, y, a, :, g] + gr2[c, 0, a, :, f].astype(F32) + gr2[c, 1, a, :, f].astype(F32) + gx[c, :, f].astype(F32)
        up = q32[c, y, :, v] + ur2[c, 0, :, v].astype(F32) + ur2[c, 1, :, v].astype(F32)
        gate = t[:, :n]
        if YF[i % 2][1] > n:
            up = jnp.concatenate([t[:, n:], up], axis=1)
        h[c, y, a, :, e] = (gate * jax.nn.sigmoid(gate) * up).astype(BF)
        own_h = h.at[c, y, a, :, e]
        send(("hx", i), own_h, own_h, across)
        send(("hr", i), own_h, own_h, right)
        send(("hl", i), own_h, own_h, left)

    def a2(i):
        got(("hx", i))
        block = h.at[i // 2, y, na, :, hid(i)]
        send(("pr", i), block, block, right)
        send(("pl", i), block, block, left)

    def a3(i):
        got(("hr", i))
        block = h.at[i // 2, yl, a, :, hid(i)]
        send(("fr", i), block, block, right)
        got(("pl", i))
        block = h.at[i // 2, yr, na, :, hid(i)]
        send(("fl", i), block, block, left)

    def m2(c):
        once(1)
        for i in (2 * c, 2 * c + 1):
            got(("hl", i), ("pr", i), ("fr", i), ("fl", i))

        def tile(j, _):
            cols = pl.ds(pl.multiple_of(j * 256, 256), 256)
            r = jnp.dot(h[c].reshape(8 * ROWS, FB), w2[:, cols], preferred_element_type=F32)
            o32[c, :, :, :, cols] = r.reshape(4, 2, ROWS, 256)
            return 0

        for half in range(2):
            lax.fori_loop(2 * half, 2 * half + 2, tile, 0)
            cols = pl.ds(512 * half, 512)
            send(("c", c, half), o32.at[c, :, 1, :, cols], cr.at[c, :, :, cols], sibling)

    def g1(c):
        got(("c", c, 0), ("c", c, 1))
        for zi in range(2):
            k = 2 * zi + 1
            zs[c, k] = (o32[c, k, 0] + cr[c, k]).astype(BF)
            send(("gh", c, zi), zs.at[c, k], zr.at[c, k], dev(dx=1))

    def g2(c):
        for zi in range(2):
            k, o = 2 * zi, OFFS[c][zi]
            got(("gh", c, zi))
            v = o32[c, k, 0] + cr[c, k] + zr[c, k + 1].astype(F32)
            if o == 0:
                own[...] = v
            else:
                source, target = (zs, zr) if o not in WIDE else (ws, wr)
                i = (c, k) if o not in WIDE else (WIDE.index(o),)
                source[i] = v.astype(source.dtype)
                send(("z", c, k), source.at[i], target.at[i], dev(dz=o))

    stages = dict(xr=xr, m1=m1, s2=s2, s3=s3, s4=s4, a2=a2, a3=a3, m2=m2, g1=g1, g2=g2)
    for i in ORDER:
        s, c = STAGES[i // 10], i % 10
        with jax.named_scope(f"{s}_{c}"):
            stages[s](c)

    total = own[...]
    for c in [i % 10 for i in ORDER if STAGES[i // 10] == "g2"]:
        for k in range(4):
            if ("z", c, k) in copies:
                got(("z", c, k))
                o = OFFS[c][k // 2]
                total += wr[WIDE.index(o)] if o in WIDE else zr[c, k].astype(F32)
    out[...] = total.astype(BF)
    for cp in copies.values():
        cp.wait_send()


def solution(mesh):
    def step(tokens, gate_weight, up_weight, down_weight):
        c = CHUNKS
        shapes = [
            ((KB, 2 * FB), BF),
            ((FB, KB), BF),
            ((c, 2, 2, 2, ROWS, KB), BF),
            ((c, 4, 2, ROWS, 2 * FB), BF),
            ((c, 4, 2, ROWS, 2 * FB), F32),
            ((c, 2, ROWS, YW), BF),
            ((c, 2, ROWS, YW), BF),
            ((c, 2, 2, ROWS, YW), BF),
            ((c, ROWS, YW), BF),
            ((c, ROWS, YW), BF),
            ((c, 4, ROWS, XW), BF),
            ((c, 4, ROWS, XW), BF),
            ((c, 4, ROWS, XW), F32),
            ((c, ROWS, XW), BF),
            ((c, ROWS, XW), BF),
            ((c, 2, ROWS, XW), BF),
            ((c, 4, 2, ROWS, FB), BF),
            ((c, 4, 2, ROWS, KB), F32),
            ((c, 4, ROWS, KB), F32),
            ((c, 4, ROWS, KB), BF),
            ((c, 4, ROWS, KB), BF),
            ((ROWS, KB), F32),
            ((len(WIDE), ROWS, KB), F32),
            ((len(WIDE), ROWS, KB), F32),
        ]
        return pl.pallas_call(
            kernel,
            name="swiglu",
            out_shape=jax.ShapeDtypeStruct((ROWS, KB), BF),
            in_specs=[pl.BlockSpec(memory_space=pl.ANY)] * 4,
            out_specs=pl.BlockSpec(memory_space=pltpu.VMEM),
            scratch_shapes=[pltpu.VMEM(s, d) for s, d in shapes]
            + [pltpu.SemaphoreType.DMA((N_SEM,)), pltpu.SemaphoreType.DMA((N_SEM,)), pltpu.SemaphoreType.DMA((6,))],
            compiler_params=pltpu.CompilerParams(collective_id=0, has_side_effects=True, vmem_limit_bytes=60 * 2**20),
        )(tokens, gate_weight, up_weight, down_weight)

    return jax.shard_map(
        step,
        mesh=mesh,
        in_specs=(
            P(("inp", "out"), "wt"),
            P("wt", ("inp", "out")),
            P("wt", ("inp", "out")),
            P(("inp", "out"), "wt"),
        ),
        out_specs=P(("inp", "out"), "wt"),
        check_vma=False,
    )
```

```python
import jax
import jax.numpy as jnp
from jax import lax
from jax.experimental import pallas as pl
from jax.experimental.pallas import tpu as pltpu
from jax.sharding import PartitionSpec as P

MESH = pl.DeviceIdType.MESH
BF, F32 = jnp.bfloat16, jnp.float32

ROWS = 48
KB = 1024
FB = 896
HID = ((0, 512), (512, 384))
COL = ((0, 1024), (1024, 768))
YF = ((0, 640), (640, 384))
XF = ((0, 384), (384, 384))
YW, XW = 1024, 768
LO = 256
CHUNKS = 4
WIDE = (1,)
OFFS = ((1, -1), (3, -3), (2, 4), (0, -2))
SLOT = {o: (c, zi) for c, pair in enumerate(OFFS) for zi, o in enumerate(pair)}
STAGES = ("xr", "m1", "s2", "s3", "s4", "a2", "a3", "m2", "g1", "g2")
ORDER = (
    2, 3, 4, 11, 5, 10, 6, 17, 21, 7, 16, 20, 13, 9, 12, 26, 31, 30, 14, 15, 41, 23, 40, 27,
    22, 25, 37, 33, 51, 32, 24, 36, 43, 50, 42, 35, 53, 52, 34, 60, 61, 47, 63, 46, 62, 45, 44, 70,
    55, 54, 57, 56, 71, 80, 65, 64, 66, 81, 67, 72, 90, 73, 82, 91, 83, 92, 93,
)
N_SEM = 240


def kernel(tok, wg, wu, wd, out, w1, w2, x, p16, p32, gr1, sb, gr2, gs, gx, ux, q16, q32, ur1, uv, ur2, h, o32, cr, zs, zr, own, ws, wr,
           ssem, rsem, lsem):
    z = lax.axis_index("inp")
    wt = lax.axis_index("wt")
    ot = lax.axis_index("out")
    a, y = wt // 4, wt % 4
    xh, core = ot // 2, ot % 2
    na = 1 - a
    yr, yl, yo = (y + 1) % 4, (y + 3) % 4, (y + 2) % 4

    def dev(dz=0, dx=0, dc=0):
        return (lax.rem(z + dz + 8, 8), wt, (xh + dx) % 2 * 2 + (core + dc) % 2)

    sibling = dev(dc=1)
    right, left, across = (z, a * 4 + yr, ot), (z, a * 4 + yl, ot), (z, na * 4 + y, ot)

    loads = [
        pltpu.make_async_copy(tok, x.at[SLOT[0] + (0, 0)], lsem.at[0]),
        pltpu.make_async_copy(wd, w2, lsem.at[1]),
    ]
    for p in range(2):
        (at, n), col = HID[p], COL[p][0]
        loads.append(pltpu.make_async_copy(wg.at[:, pl.ds(at, n)], w1.at[:, pl.ds(col, n)], lsem.at[2 + 2 * p]))
        loads.append(pltpu.make_async_copy(wu.at[:, pl.ds(at, n)], w1.at[:, pl.ds(col + n, n)], lsem.at[3 + 2 * p]))
    for load in loads:
        load.start()

    barrier = pltpu.get_barrier_semaphore()
    peers = [sibling, right, left, across, dev(dx=1), dev(dz=1), dev(dz=-1)]
    for peer in peers:
        pl.semaphore_signal(barrier, inc=1, device_id=peer, device_id_type=MESH)
    pl.semaphore_wait(barrier, len(peers))

    copies = {}

    def send(name, src, dst, to):
        i = len(copies)
        cp = pltpu.make_async_remote_copy(
            src_ref=src, dst_ref=dst, send_sem=ssem.at[i], recv_sem=rsem.at[i], device_id=to, device_id_type=MESH
        )
        cp.start()
        copies[name] = cp

    def got(*names):
        for name in names:
            copies[name].wait_recv()

    def xs(o, rx, rc):
        return x.at[SLOT[o] + (rx, rc)]

    def hop(k, rx, step):
        o = k - step
        o = 4 if o == -4 else o
        send(("x", o, rx), xs(k, rx, 0), xs(o, rx, 0), dev(dz=step))

    loads[0].wait()
    hop(0, 0, 1)
    hop(0, 0, -1)
    send("x_hi", xs(0, 0, 0), xs(0, 1, 0), dev(dx=1))
    send("x_c0", xs(0, 0, 0), xs(0, 0, 1), sibling)
    got("x_hi")
    hop(0, 1, 1)
    hop(0, 1, -1)
    send("x_c1", xs(0, 1, 0), xs(0, 1, 1), sibling)

    def to_sibling(o):
        c, zi = SLOT[o]
        send(("xc", o), x.at[c, zi, :, 0], x.at[c, zi, :, 1], sibling)

    def xr(k):
        k, rx = k // 2, k % 2
        if k == 4:
            got(("x", 4, 0), ("x", 4, 1))
            to_sibling(4)
            return
        got(("x", -k, rx))
        if k < 3 or rx == 0:
            hop(-k, rx, 1)
        got(("x", k, rx))
        if k < 3 or rx == 1:
            hop(k, rx, -1)
        if rx == 1:
            to_sibling(k)
            to_sibling(-k)

    waited = set()

    def once(*which):
        for i in which:
            if i not in waited:
                waited.add(i)
                loads[i].wait()

    def yf(i, at=0, n=None):
        return pl.ds(YF[i % 2][0] + at, YF[i % 2][1] - at if n is None else n)

    def xf(i, at=0, n=None):
        return pl.ds(XF[i % 2][0] + at, XF[i % 2][1] - at if n is None else n)

    def pcols(i):
        col, width = COL[i % 2]
        n = YF[i % 2][1]
        return pl.ds(col, n), pl.ds(col + n, width - n)

    def hid(i):
        return pl.ds(*HID[i % 2])

    def m1(i):
        c, p = i // 2, i % 2
        once(2 + 2 * p, 3 + 2 * p)
        for o in OFFS[c]:
            if ("xo", o) not in waited:
                waited.add(("xo", o))
                if o:
                    got(("xc", o))
                else:
                    got("x_c0", "x_c1")

        def tile(j, _):
            cols = pl.ds(pl.multiple_of(COL[p][0] + j * 256, 256), 256)
            r = jnp.dot(x[c].reshape(8 * ROWS, KB), w1[:, cols], preferred_element_type=F32)
            r = r.reshape(4, 2, ROWS, 256)
            p32[c, :, :, :, cols] = r
            p16[c, :, :, :, cols] = r.astype(BF)
            return 0

        lax.fori_loop(0, COL[p][1] // 256, tile, 0)
        g, u = pcols(i)
        send(("u0", i), p16.at[c, :, na, :, u], ux.at[c, :, :, xf(i)], across)
        send(("g1r", i), p16.at[c, yo, 0, :, g], gr1.at[c, 0, :, yf(i)], right)
        send(("g1l", i), p16.at[c, yo, 1, :, g], gr1.at[c, 1, :, yf(i)], left)
        send(("g2r1", i), p16.at[c, yr, 1, :, g], gr2.at[c, 0, 1, :, yf(i)], right)
        send(("g2l0", i), p16.at[c, yl, 0, :, g], gr2.at[c, 1, 0, :, yf(i)], left)

    def s2(i):
        c = i // 2
        g, u = pcols(i)
        f, v = yf(i), xf(i)
        got(("g1r", i))
        sb[c, 0, :, f] = (p32[c, yr, 0, :, g] + gr1[c, 0, :, f].astype(F32)).astype(BF)
        send(("g2r0", i), sb.at[c, 0, :, f], gr2.at[c, 0, 0, :, f], right)
        got(("g1l", i))
        sb[c, 1, :, f] = (p32[c, yl, 1, :, g] + gr1[c, 1, :, f].astype(F32)).astype(BF)
        send(("g2l1", i), sb.at[c, 1, :, f], gr2.at[c, 1, 1, :, f], left)
        got(("u0", i))
        for k in range(4):
            q = p32[c, k, a, :, u] + ux[c, k, :, v].astype(F32)
            q32[c, k, :, v] = q
            q16[c, k, :, v] = q.astype(BF)
        lo, hi = xf(i, 0, LO), xf(i, LO)
        send(("u1r", i), q16.at[c, yo, :, lo], ur1.at[c, :, lo], right)
        send(("u1l", i), q16.at[c, yo, :, hi], ur1.at[c, :, hi], left)
        send(("u2rh", i), q16.at[c, yr, :, hi], ur2.at[c, 0, :, hi], right)
        send(("u2ll", i), q16.at[c, yl, :, lo], ur2.at[c, 1, :, lo], left)

    def s3(i):
        c = i // 2
        g, _ = pcols(i)
        f = yf(i)
        got(("g2r0", i), ("g2r1", i), ("g2l0", i), ("g2l1", i))
        t = p32[c, y, na, :, g] + gr2[c, 0, na, :, f].astype(F32) + gr2[c, 1, na, :, f].astype(F32)
        gs[c, :, f] = t.astype(BF)
        send(("gx", i), gs.at[c, :, f], gx.at[c, :, f], across)
        lo, hi = xf(i, 0, LO), xf(i, LO)
        got(("u1r", i))
        uv[c, :, lo] = (q32[c, yr, :, lo] + ur1[c, :, lo].astype(F32)).astype(BF)
        send(("u2rl", i), uv.at[c, :, lo], ur2.at[c, 0, :, lo], right)
        got(("u1l", i))
        uv[c, :, hi] = (q32[c, yl, :, hi] + ur1[c, :, hi].astype(F32)).astype(BF)
        send(("u2lh", i), uv.at[c, :, hi], ur2.at[c, 1, :, hi], left)

    def s4(i):
        c = i // 2
        g, _ = pcols(i)
        f, v, e = yf(i), xf(i), hid(i)
        n = HID[i % 2][1]
        got(("gx", i), ("u2rl", i), ("u2rh", i), ("u2ll", i), ("u2lh", i))
        t = p32[c, y, a, :, g] + gr2[c, 0, a, :, f].astype(F32) + gr2[c, 1, a, :, f].astype(F32) + gx[c, :, f].astype(F32)
        up = q32[c, y, :, v] + ur2[c, 0, :, v].astype(F32) + ur2[c, 1, :, v].astype(F32)
        gate = t[:, :n]
        if YF[i % 2][1] > n:
            up = jnp.concatenate([t[:, n:], up], axis=1)
        h[c, y, a, :, e] = (gate * jax.nn.sigmoid(gate) * up).astype(BF)
        own_h = h.at[c, y, a, :, e]
        send(("hx", i), own_h, own_h, across)
        send(("hr", i), own_h, own_h, right)
        send(("hl", i), own_h, own_h, left)

    def a2(i):
        got(("hx", i))
        block = h.at[i // 2, y, na, :, hid(i)]
        send(("pr", i), block, block, right)
        send(("pl", i), block, block, left)

    def a3(i):
        got(("hr", i))
        block = h.at[i // 2, yl, a, :, hid(i)]
        send(("fr", i), block, block, right)
        got(("pl", i))
        block = h.at[i // 2, yr, na, :, hid(i)]
        send(("fl", i), block, block, left)

    def m2(c):
        once(1)
        for i in (2 * c, 2 * c + 1):
            got(("hl", i), ("pr", i), ("fr", i), ("fl", i))

        def tile(j, _):
            cols = pl.ds(pl.multiple_of(j * 256, 256), 256)
            r = jnp.dot(h[c].reshape(8 * ROWS, FB), w2[:, cols], preferred_element_type=F32)
            o32[c, :, :, :, cols] = r.reshape(4, 2, ROWS, 256)
            return 0

        for half in range(2):
            lax.fori_loop(2 * half, 2 * half + 2, tile, 0)
            cols = pl.ds(512 * half, 512)
            send(("c", c, half), o32.at[c, :, 1, :, cols], cr.at[c, :, :, cols], sibling)

    def g1(c):
        got(("c", c, 0), ("c", c, 1))
        for zi in range(2):
            k = 2 * zi + 1
            zs[c, k] = (o32[c, k, 0] + cr[c, k]).astype(BF)
            send(("gh", c, zi), zs.at[c, k], zr.at[c, k], dev(dx=1))

    def g2(c):
        for zi in range(2):
            k, o = 2 * zi, OFFS[c][zi]
            got(("gh", c, zi))
            v = o32[c, k, 0] + cr[c, k] + zr[c, k + 1].astype(F32)
            if o == 0:
                own[...] = v
            else:
                source, target = (zs, zr) if o not in WIDE else (ws, wr)
                i = (c, k) if o not in WIDE else (WIDE.index(o),)
                source[i] = v.astype(source.dtype)
                send(("z", c, k), source.at[i], target.at[i], dev(dz=o))

    stages = dict(xr=xr, m1=m1, s2=s2, s3=s3, s4=s4, a2=a2, a3=a3, m2=m2, g1=g1, g2=g2)
    for i in ORDER:
        s, c = STAGES[i // 10], i % 10
        with jax.named_scope(f"{s}_{c}"):
            stages[s](c)

    total = own[...]
    for c in [i % 10 for i in ORDER if STAGES[i // 10] == "g2"]:
        for k in range(4):
            if ("z", c, k) in copies:
                got(("z", c, k))
                o = OFFS[c][k // 2]
                total += wr[WIDE.index(o)] if o in WIDE else zr[c, k].astype(F32)
    out[...] = total.astype(BF)
    for cp in copies.values():
        cp.wait_send()


def solution(mesh):
    def step(tokens, gate_weight, up_weight, down_weight):
        c = CHUNKS
        shapes = [
            ((KB, 2 * FB), BF),
            ((FB, KB), BF),
            ((c, 2, 2, 2, ROWS, KB), BF),
            ((c, 4, 2, ROWS, 2 * FB), BF),
            ((c, 4, 2, ROWS, 2 * FB), F32),
            ((c, 2, ROWS, YW), BF),
            ((c, 2, ROWS, YW), BF),
            ((c, 2, 2, ROWS, YW), BF),
            ((c, ROWS, YW), BF),
            ((c, ROWS, YW), BF),
            ((c, 4, ROWS, XW), BF),
            ((c, 4, ROWS, XW), BF),
            ((c, 4, ROWS, XW), F32),
            ((c, ROWS, XW), BF),
            ((c, ROWS, XW), BF),
            ((c, 2, ROWS, XW), BF),
            ((c, 4, 2, ROWS, FB), BF),
            ((c, 4, 2, ROWS, KB), F32),
            ((c, 4, ROWS, KB), F32),
            ((c, 4, ROWS, KB), BF),
            ((c, 4, ROWS, KB), BF),
            ((ROWS, KB), F32),
            ((len(WIDE), ROWS, KB), F32),
            ((len(WIDE), ROWS, KB), F32),
        ]
        return pl.pallas_call(
            kernel,
            name="swiglu",
            out_shape=jax.ShapeDtypeStruct((ROWS, KB), BF),
            in_specs=[pl.BlockSpec(memory_space=pl.ANY)] * 4,
            out_specs=pl.BlockSpec(memory_space=pltpu.VMEM),
            scratch_shapes=[pltpu.VMEM(s, d) for s, d in shapes]
            + [pltpu.SemaphoreType.DMA((N_SEM,)), pltpu.SemaphoreType.DMA((N_SEM,)), pltpu.SemaphoreType.DMA((6,))],
            compiler_params=pltpu.CompilerParams(collective_id=0, has_side_effects=True, vmem_limit_bytes=60 * 2**20),
        )(tokens, gate_weight, up_weight, down_weight)

    return jax.shard_map(
        step,
        mesh=mesh,
        in_specs=(
            P(("inp", "out"), "wt"),
            P("wt", ("inp", "out")),
            P("wt", ("inp", "out")),
            P(("inp", "out"), "wt"),
        ),
        out_specs=P(("inp", "out"), "wt"),
        check_vma=False,
    )
```
